32 devices in a mesh: row: 4 (over z), col: 8 (over y, x, core).
Axes of the slice: x: 2, y: 2, z: 4, core: 2. Of those that a mesh axis runs over, the one named last changes fastest.
Arguments:
- features: bfloat16 [65536, 256], P(('row', 'col')), may hold values from -6 to 6
- cotangent: bfloat16 [65536, 256], P(('row', 'col')), may hold values from -6 to 6
- tile_values: bfloat16 [512, 4, 4, 128, 128], P(('row', 'col')), may hold values from -0.25 to 0.25
- tile_src: int32 [512, 4, 4], P(('row', 'col')), may hold values from 0 to 17
- tile_count: int32 [512, 4], P(('row', 'col')), may hold values from 1 to 4
- send_rows: int32 [32, 32, 8], P(('row', 'col')), may hold values from 0 to 2047
- w_stack: bfloat16 [1280, 256], replicated, may hold values from -0.375 to 0.375
- w_qkv: bfloat16 [256, 768], replicated, may hold values from -0.375 to 0.375
Outputs:
- layer_out: bfloat16 [65536, 256], P(('row', 'col'))
- input_grad: bfloat16 [65536, 256], P(('row', 'col'))
- stack_grad: float32 [1280, 256], replicated
- qkv_grad: float32 [256, 768], replicated
The draws below stay inside these ranges and needn't reach their ends.
Inputs may be any that keep to these rules, and one draw needn't show every extreme that they name: `tile_src`: a tile of the partition's own rows (below 16) or of its received boundary rows. `send_rows`: a row of the sending partition.
All inputs are finite; a program needn't handle non-finite values.
Results may differ from the reference program's by a relative error of at most 0.0061.
Values may be sent and summed in bfloat16 or wider, within the bound.
A program may use at most 128 MiB of HBM per device.

```python
import jax
import jax.numpy as jnp
from jax import lax

H = 256
HEADS = 4
RELS = 4
TILE = 128
TPR = 4
NODE_DEV = 2048
BND = 8
HD = 64
NT = 16
NT_EXT = 18
NODES = 65536
NTILES = 512
DEVICES = 32


def plant(result, own_key, smallest, high):
    spot = [jax.random.randint(jax.random.fold_in(own_key, axis), (), 0, length) for axis, length in enumerate(result.shape)]
    widest = result.shape.index(max(result.shape))
    neighbour = spot[:widest] + [(spot[widest] + 1) % result.shape[widest]] + spot[widest + 1:]
    return result.at[tuple(spot)].set(smallest).at[tuple(neighbour)].set(high)


def shard_levels(stream_key, dims, shards, smallest, high):
    factor_of, own = 1.0, jax.random.fold_in(stream_key, 6)
    for axis_at, parts in shards:
        heights = jnp.exp(jax.random.uniform(jax.random.fold_in(own, axis_at), (parts,), jnp.float32, smallest / len(shards), high / len(shards)))
        factor_of = factor_of * jnp.repeat(heights, dims[axis_at] // parts).reshape([-1 if axis == axis_at else 1 for axis in range(len(dims))])
    return factor_of


def bell_draw(stream_key, extent, width, reach, shards=(), kind=jnp.bfloat16):
    values = width * jax.random.normal(stream_key, extent, jnp.float32)
    if shards:
        values = values * shard_levels(stream_key, extent, shards, -0.22, 0.18)
    return jnp.clip(values, -reach, reach).astype(kind)


def setup_inputs(seed: int = 0) -> dict:
    streams_of = jax.random.split(jax.random.key(seed), 9)
    return {
        "features": bell_draw(streams_of[0], (NODES, H), 1.0, 6.0, ((0, 32),)),
        "cotangent": bell_draw(streams_of[1], (NODES, H), 1.0, 6.0, ((0, 32),)),
        "tile_values": bell_draw(streams_of[2], (NTILES, RELS, TPR, TILE, TILE), (TILE * TPR) ** -0.5, 0.25, ((0, 32),)),
        "tile_src": plant(jax.random.randint(streams_of[3], (NTILES, RELS, TPR), 0, NT_EXT), jax.random.fold_in(streams_of[3], 1), 0, NT_EXT - 1).astype(jnp.int32),
        "tile_count": plant(jax.random.randint(streams_of[4], (NTILES, RELS), 1, TPR + 1), jax.random.fold_in(streams_of[4], 1), 1, TPR).astype(jnp.int32),
        "send_rows": plant(jax.random.randint(streams_of[5], (DEVICES, DEVICES, BND), 0, NODE_DEV), jax.random.fold_in(streams_of[5], 1), 0, NODE_DEV - 1).astype(jnp.int32),
        "w_stack": bell_draw(streams_of[6], ((RELS + 1) * H, H), H ** -0.5, 0.375),
        "w_qkv": bell_draw(streams_of[7], (H, 3 * H), H ** -0.5, 0.375),
    }


def slot_mask(values, source, counts):
    slots = lax.broadcasted_iota(jnp.int32, source.shape, source.ndim - 1)
    active = slots < counts[..., None]
    return jnp.where(active[..., None, None], values, jnp.zeros((), values.dtype))

def forward_device(inputs):
    extended, values, source, counts = inputs
    masked = slot_mask(values, source, counts)
    picked = extended[source]
    messages = jnp.einsum('trsij,trsjh->tirh', masked.astype(jnp.float32), picked.astype(jnp.float32))
    return messages.astype(jnp.bfloat16)

def backward_device(inputs):
    values, source, counts, pulled = inputs
    masked = slot_mask(values, source, counts)
    spread = jnp.einsum('trsij,tirh->trsjh', masked.astype(jnp.float32), pulled.astype(jnp.float32))
    targets = lax.broadcasted_iota(jnp.int32, (1, 1, 1, NT_EXT), 3)
    one_hot = (source[..., None] == targets).astype(jnp.float32)
    return jnp.einsum('trse,trsjh->ejh', one_hot, spread, precision=lax.Precision.HIGHEST)

def reference(features, cotangent, tile_values, tile_src, tile_count, send_rows, w_stack, w_qkv):
    devices = send_rows.shape[0]
    local = features.reshape(devices, NODE_DEV, H)
    flat_rows = send_rows.reshape(devices, devices * BND).astype(jnp.int32)
    picked = jax.vmap(lambda source, indices: source[indices])(local, flat_rows)
    halo = picked.reshape(devices, devices, BND, H).transpose(1, 0, 2, 3).reshape(devices, devices * BND, H)
    extended = jnp.concatenate([local, halo], axis=1).reshape(devices, NT_EXT, TILE, H)
    values = tile_values.reshape(devices, NT, RELS, TPR, TILE, TILE)
    source = tile_src.reshape(devices, NT, RELS, TPR).astype(jnp.int32)
    counts = tile_count.reshape(devices, NT, RELS).astype(jnp.int32)
    messages = lax.map(forward_device, (extended, values, source, counts))
    messages = messages.reshape(NODES, RELS * H)
    joined = jnp.concatenate([features, messages], axis=1)
    pre = jnp.dot(joined, w_stack, preferred_element_type=jnp.float32)
    qkv = jnp.dot(features, w_qkv, preferred_element_type=jnp.float32).astype(jnp.bfloat16)
    query = qkv[:, :H].astype(jnp.float32).reshape(NODES, HEADS, HD)
    keys = qkv[:, H:2 * H].astype(jnp.float32).reshape(NODES, HEADS, HD)
    vals = qkv[:, 2 * H:].astype(jnp.float32).reshape(NODES, HEADS, HD)
    node_scale = 1.0 / jnp.sqrt(jnp.float32(NODES))
    head_scale = 1.0 / jnp.sqrt(jnp.float32(HD))
    kv_state = jnp.einsum('nha,nhb->hab', keys, vals, precision=lax.Precision.HIGHEST) * node_scale
    attended = jnp.einsum('nha,hab->nhb', query, kv_state, precision=lax.Precision.HIGHEST) * head_scale
    activated, pull_back = jax.vjp(jax.nn.gelu, pre)
    layer_out = (activated + attended.reshape(NODES, H)).astype(jnp.bfloat16)
    grad_out = cotangent.astype(jnp.float32)
    grad_pre = pull_back(grad_out)[0].astype(jnp.bfloat16)
    grad_back = lax.dot_general(grad_pre, w_stack, (((1,), (1,)), ((), ())), preferred_element_type=jnp.float32)
    self_back = grad_back[:, :H]
    pulled = grad_back[:, H:].astype(jnp.bfloat16).reshape(devices, NT, TILE, RELS, H)
    ext_grad = lax.map(backward_device, (values, source, counts, pulled))
    local_grad = ext_grad[:, :NT].reshape(NODES, H)
    halo_grad = ext_grad[:, NT:].reshape(devices, devices, BND, H).astype(jnp.bfloat16)
    returned = halo_grad.transpose(1, 0, 2, 3).reshape(devices, devices * BND, H).astype(jnp.float32)
    scattered = jax.vmap(lambda indices, addend: jnp.zeros((NODE_DEV, H), jnp.float32).at[indices].add(addend))(flat_rows, returned)
    gcn_grad = self_back + local_grad + scattered.reshape(NODES, H)
    grad_heads = grad_out.reshape(NODES, HEADS, HD)
    state_grad = jnp.einsum('nha,nhb->hab', query, grad_heads, precision=lax.Precision.HIGHEST) * head_scale
    grad_query = jnp.einsum('nhb,hab->nha', grad_heads, kv_state, precision=lax.Precision.HIGHEST) * head_scale
    grad_keys = jnp.einsum('nhb,hab->nha', vals, state_grad, precision=lax.Precision.HIGHEST) * node_scale
    grad_vals = jnp.einsum('nha,hab->nhb', keys, state_grad, precision=lax.Precision.HIGHEST) * node_scale
    dqkv = jnp.concatenate([grad_query.reshape(NODES, H), grad_keys.reshape(NODES, H), grad_vals.reshape(NODES, H)], axis=1)
    dqkv_low = dqkv.astype(jnp.bfloat16)
    stack_grad = lax.dot_general(joined, grad_pre, (((0,), (0,)), ((), ())), preferred_element_type=jnp.float32)
    qkv_grad = lax.dot_general(features.astype(jnp.float32), dqkv, (((0,), (0,)), ((), ())), precision=lax.Precision.HIGHEST)
    attn_back = lax.dot_general(dqkv_low, w_qkv, (((1,), (1,)), ((), ())), preferred_element_type=jnp.float32)
    input_grad = (gcn_grad + attn_back).astype(jnp.bfloat16)
    return (layer_out, input_grad, stack_grad, qkv_grad)
```

```python
import functools

import jax
import jax.numpy as jnp
from jax import lax
from jax.experimental import pallas as pl
from jax.experimental.pallas import tpu as pltpu
from jax.sharding import PartitionSpec as P

HEADS = 4
RELS = 4
TILE = 128
MESH = pl.DeviceIdType.MESH
BF16 = jnp.bfloat16
F32 = jnp.float32
VMEM_LIMIT = 48 * 1024 * 1024
STEP_TILES = 2


def dot(a, b, dims=((1,), (0,)), precision=None):
    return lax.dot_general(a, b, (dims, ((), ())), preferred_element_type=F32, precision=precision)


def pack_rows(rows, bound):
    count, width = rows.shape
    left = rows[:, : width // 2].reshape(count // bound, bound, width // 2)
    right = rows[:, width // 2 :].reshape(count // bound, bound, width // 2)
    return jnp.concatenate([left, right], axis=1)


def unpack_rows(packed, bound):
    count, _, half = packed.shape
    left = packed[:, :bound].reshape(count * bound, half)
    right = packed[:, bound:].reshape(count * bound, half)
    return jnp.concatenate([left, right], axis=1)


class Place:
    def __init__(self, rows, cols):
        self.rows, self.cols, self.planes = rows, cols, cols // 2
        self.devices = rows * cols
        self.row, self.col = lax.axis_index("row"), lax.axis_index("col")
        self.me = self.row * cols + self.col
        self.core = lax.rem(self.col, 2)
        self.plane = lax.div(self.col, 2)

    def peer(self, offset):
        other = lax.rem(self.me + offset, self.devices)
        return (lax.div(other, self.cols), lax.rem(other, self.cols))

    def greet(self):
        barrier = pltpu.get_barrier_semaphore()

        def signal(offset, carry):
            pl.semaphore_signal(barrier, inc=1, device_id=self.peer(offset), device_id_type=MESH)
            return carry

        lax.fori_loop(1, self.devices, signal, 0)

    def met(self):
        pl.semaphore_wait(pltpu.get_barrier_semaphore(), self.devices - 1)


def exchange_copy(place, offset, out, into, sends, recvs):
    other = lax.rem(place.me + offset, place.devices)
    return pltpu.make_async_remote_copy(
        src_ref=out.at[other],
        dst_ref=into.at[place.me],
        send_sem=sends.at[offset],
        recv_sem=recvs.at[offset],
        device_id=place.peer(offset),
        device_id_type=MESH,
    )


def exchange_start(place, out, into, sends, recvs):
    into[place.me] = out[place.me]

    def start(offset, carry):
        exchange_copy(place, offset, out, into, sends, recvs).start()
        return carry

    lax.fori_loop(1, place.devices, start, 0)


def exchange_wait(place, out, into, sends, recvs):
    def wait(offset, carry):
        exchange_copy(place, offset, out, into, sends, recvs).wait()
        return carry

    lax.fori_loop(1, place.devices, wait, 0)


def sum_scratch(rows, width, row_count, col_count):
    half, chunk, planes = rows // 2, rows // col_count, col_count // 2
    count = 1 + 2 * (planes - 1) + (row_count - 1) + planes
    return [
        pltpu.VMEM((half, width), BF16),
        pltpu.VMEM((half, width), BF16),
        pltpu.VMEM((half, width), BF16),
        pltpu.VMEM((planes, chunk, width), BF16),
        pltpu.VMEM((row_count, chunk, width), BF16),
        pltpu.SemaphoreType.DMA((count,)),
        pltpu.SemaphoreType.DMA((count,)),
    ]


def sum_all(place, part, out, scratch):
    out0, in0, out1, in1, in2, sends, recvs = scratch
    rows = part.shape[0]
    half, chunk = rows // 2, rows // place.cols
    core, plane, row, planes = place.core, place.plane, place.row, place.planes
    partner = (row, place.col + 1 - 2 * core)
    used = [0]

    def copy(src, dst, device):
        index = used[0]
        used[0] += 1
        return pltpu.make_async_remote_copy(
            src_ref=src, dst_ref=dst, send_sem=sends.at[index], recv_sem=recvs.at[index],
            device_id=device, device_id_type=MESH,
        )

    out0[...] = part[pl.ds(pl.multiple_of((1 - core) * half, 16), half), :].astype(BF16)
    first = copy(out0, in0, partner)
    first.start()
    first.wait()
    mine = part[pl.ds(pl.multiple_of(core * half, 16), half), :]
    out1[...] = (mine + in0[...].astype(F32)).astype(BF16)

    def piece(index):
        return pl.ds(pl.multiple_of(index * chunk, 16), chunk)

    copies = []
    for step in range(1, planes):
        other = lax.rem(plane + step, planes)
        moved = copy(out1.at[piece(other), :], in1.at[step], (row, other * 2 + core))
        moved.start()
        copies.append(moved)
    total = out1[piece(plane), :].astype(F32)
    for step in range(1, planes):
        copies[step - 1].wait()
        total = total + in1[step].astype(F32)

    in2[row] = total.astype(BF16)
    copies = []
    for step in range(1, place.rows):
        other = lax.rem(row + step, place.rows)
        moved = copy(in2.at[row], in2.at[row], (other, place.col))
        moved.start()
        copies.append(moved)
    for moved in copies:
        moved.wait()
    total = in2[0].astype(F32)
    for step in range(1, place.rows):
        total = total + in2[step].astype(F32)

    def spot(index):
        return pl.ds(pl.multiple_of(core * half + index * chunk, 16), chunk)

    out[spot(plane), :] = total.astype(BF16)
    copies, passed = [], []
    for step in range(1, planes):
        other = lax.rem(plane + step, planes)
        moved = copy(out.at[spot(plane), :], out.at[spot(plane), :], (row, other * 2 + core))
        moved.start()
        copies.append(moved)
    moved = copy(out.at[spot(plane), :], out.at[spot(plane), :], partner)
    moved.start()
    passed.append(moved)
    for step in range(1, planes):
        copies[step - 1].wait()
        source = spot(lax.rem(plane - step + planes, planes))
        moved = copy(out.at[source, :], out.at[source, :], partner)
        moved.start()
        passed.append(moved)
    for moved in passed:
        moved.wait()


def gather_kernel(shape, f_ref, c_ref, rows_ref, halo_ref, moments_ref, outgoing, incoming, sends, recvs, part, *scratch):
    row_count, col_count, bound = shape
    place = Place(row_count, col_count)
    place.greet()
    nodes, width = f_ref.shape
    block = 512
    wanted = rows_ref[...]
    picked = jnp.zeros((wanted.shape[0], width), F32)
    for at in range(0, nodes, block):
        spots = lax.broadcasted_iota(jnp.int32, (wanted.shape[0], block), 1) + at
        picked += dot(jnp.where(spots == wanted, 1.0, 0.0).astype(BF16), f_ref[at : at + block, :])
    outgoing[...] = pack_rows(picked, bound).astype(BF16)
    place.met()
    exchange_start(place, outgoing, incoming, sends, recvs)
    gram = jnp.zeros((width, width), F32)
    cross = jnp.zeros((width, width), F32)
    for at in range(0, nodes, block):
        f = f_ref[at : at + block, :]
        gram += dot(f, f, ((0,), (0,)))
        cross += dot(f, c_ref[at : at + block, :], ((0,), (0,)))
    part[:width, :] = gram
    part[width:, :] = cross
    sum_all(place, part, moments_ref, scratch)
    exchange_wait(place, outgoing, incoming, sends, recvs)
    halo_ref[...] = unpack_rows(incoming[...].astype(F32), bound).astype(BF16)


def layer_kernel(
    scales, bound, index_ref, f_ref, c_ref, halo_ref, moments_ref, w_ref, wqkv_ref, tv_ref,
    out_ref, stack_ref, local_ref, back_ref, qkv_ref, ext, ext_grad, joined, mix, sym,
):
    node_scale, head_scale = scales
    step = pl.program_id(0)
    nodes, width = f_ref.shape
    tiles = nodes // TILE
    span = ext.shape[0] - 1
    head = width // HEADS
    highest = lax.Precision.HIGHEST

    @pl.when(step == 0)
    def _():
        for t in range(tiles):
            ext[t] = f_ref[t * TILE : (t + 1) * TILE, :]
        for t in range(tiles, span):
            ext[t] = halo_ref[(t - tiles) * TILE : (t - tiles + 1) * TILE, :]
        ext[span] = jnp.zeros((TILE, width), BF16)
        ext_grad[...] = jnp.zeros_like(ext_grad)
        stack_ref[...] = jnp.zeros_like(stack_ref)
        gram = moments_ref[:width, :].astype(F32)
        cross = moments_ref[width:, :].astype(F32)
        w_q = wqkv_ref[:, :width].astype(F32)
        w_k = wqkv_ref[:, width : 2 * width].astype(F32)
        w_v = wqkv_ref[:, 2 * width :].astype(F32)
        same = lax.div(lax.broadcasted_iota(jnp.int32, (width, width), 0), head) == lax.div(
            lax.broadcasted_iota(jnp.int32, (width, width), 1), head
        )
        gram_v = dot(gram, w_v, precision=highest)
        gram_k = dot(gram, w_k, precision=highest)
        state = jnp.where(same, dot(w_k, gram_v, ((0,), (0,)), highest), 0.0) * node_scale
        state_grad = jnp.where(same, dot(w_q, cross, ((0,), (0,)), highest), 0.0) * head_scale
        mix[...] = (dot(w_q, state, precision=highest) * head_scale).astype(BF16)
        turned = dot(dot(w_k, state_grad, precision=highest), w_v, ((1,), (1,)), highest)
        sym[...] = ((turned + turned.T) * node_scale).astype(BF16)
        qkv_ref[:, :width] = dot(cross, state, ((1,), (1,)), highest) * head_scale
        qkv_ref[:, width : 2 * width] = dot(gram_v, state_grad, ((1,), (1,)), highest) * node_scale
        qkv_ref[:, 2 * width :] = dot(gram_k, state_grad, precision=highest) * node_scale

    rows = STEP_TILES * TILE
    here = pl.ds(pl.multiple_of(step * rows, rows), rows)
    feats, cots = f_ref[here, :], c_ref[here, :]
    joined[:, :width] = feats

    def slot(tile, relation, s):
        return index_ref[((step * STEP_TILES + tile) * RELS + relation) * 4 + s]

    def adjacency(tile, relation):
        return jnp.concatenate([tv_ref[tile, relation, s] for s in range(4)], axis=1)

    for tile in range(STEP_TILES):
        for relation in range(RELS):
            source = jnp.concatenate([ext[slot(tile, relation, s)] for s in range(4)], axis=0)
            message = dot(adjacency(tile, relation), source)
            joined[tile * TILE : (tile + 1) * TILE, (relation + 1) * width : (relation + 2) * width] = message.astype(BF16)
    pre = dot(joined[...], w_ref[...])
    root = 0.7978845608028654
    square = pre * pre
    bent = jnp.tanh(root * pre * (1.0 + 0.044715 * square))
    upper = 0.5 * (1.0 + bent)
    slope = upper + 0.5 * pre * (1.0 - bent * bent) * root * (1.0 + 3 * 0.044715 * square)
    grad_pre = (cots.astype(F32) * slope).astype(BF16)
    out_ref[...] = (pre * upper + dot(feats, mix[...])).astype(BF16)
    stack_ref[...] += dot(joined[...], grad_pre, ((0,), (0,)))
    own = (
        dot(w_ref[:width, :], grad_pre, ((1,), (1,)))
        + dot(mix[...], cots, ((1,), (1,)))
        + dot(sym[...], feats, ((1,), (1,)))
    )
    for tile in range(STEP_TILES):
        ext_grad[step * STEP_TILES + tile] += own[:, tile * TILE : (tile + 1) * TILE]
    for relation in range(RELS):
        pulled = dot(w_ref[(relation + 1) * width : (relation + 2) * width, :], grad_pre, ((1,), (1,))).astype(BF16)
        for tile in range(STEP_TILES):
            spread = dot(pulled[:, tile * TILE : (tile + 1) * TILE], adjacency(tile, relation))
            for s in range(4):
                ext_grad[slot(tile, relation, s)] += spread[:, s * TILE : (s + 1) * TILE]

    @pl.when(step == pl.num_programs(0) - 1)
    def _():
        for t in range(tiles):
            local_ref[t * TILE : (t + 1) * TILE, :] = ext_grad[t].T
        group = TILE // bound
        for t in range(tiles, span):
            back_ref[(t - tiles) * group : (t - tiles + 1) * group] = pack_rows(ext_grad[t].T, bound).astype(BF16)


def return_kernel(shape, stack_in, back_in, local_in, rows_ref, stack_ref, grad_ref, incoming, sends, recvs, total, *scratch):
    row_count, col_count, bound = shape
    place = Place(row_count, col_count)
    place.greet()
    place.met()
    exchange_start(place, back_in, incoming, sends, recvs)
    sum_all(place, stack_in, total, scratch)
    stack_ref[...] = total[...].astype(F32)
    exchange_wait(place, back_in, incoming, sends, recvs)
    returned = unpack_rows(incoming[...].astype(F32), bound).astype(BF16)
    nodes = local_in.shape[0]
    wanted = rows_ref[...]
    block = 512
    for at in range(0, nodes, block):
        spots = lax.broadcasted_iota(jnp.int32, (block, wanted.shape[1]), 0) + at
        spread = dot(jnp.where(spots == wanted, 1.0, 0.0).astype(BF16), returned)
        grad_ref[at : at + block, :] = (local_in[at : at + block, :] + spread).astype(BF16)


def local(row_count, col_count, features, cotangent, tile_values, tile_src, tile_count, send_rows, w_stack, w_qkv):
    nodes, width = features.shape
    devices = row_count * col_count
    bound = send_rows.shape[2]
    tiles = nodes // TILE
    span = tiles + devices * bound // TILE
    slots = lax.broadcasted_iota(jnp.int32, tile_src.shape, 2)
    index = jnp.where(slots < tile_count[:, :, None], tile_src, span).reshape(-1)
    shape = (row_count, col_count, bound)
    in_vmem = pl.BlockSpec(memory_space=pltpu.VMEM)
    packed = (devices, 2 * bound, width // 2)

    halo, moments = pl.pallas_call(
        functools.partial(gather_kernel, shape),
        out_shape=(
            jax.ShapeDtypeStruct((devices * bound, width), BF16),
            jax.ShapeDtypeStruct((2 * width, width), BF16),
        ),
        in_specs=[in_vmem] * 3,
        out_specs=(in_vmem, in_vmem),
        scratch_shapes=[
            pltpu.VMEM(packed, BF16),
            pltpu.VMEM(packed, BF16),
            pltpu.SemaphoreType.DMA((devices,)),
            pltpu.SemaphoreType.DMA((devices,)),
            pltpu.VMEM((2 * width, width), F32),
            *sum_scratch(2 * width, width, row_count, col_count),
        ],
        compiler_params=pltpu.CompilerParams(
            collective_id=0, has_side_effects=True, vmem_limit_bytes=VMEM_LIMIT
        ),
        name="gather",
    )(features, cotangent, send_rows.reshape(devices * bound, 1))

    rows = STEP_TILES * TILE
    whole = lambda *dims: pl.BlockSpec(dims, lambda i, index: (0,) * len(dims))
    scales = (float(nodes * devices) ** -0.5, float(width // HEADS) ** -0.5)
    stack = w_stack.shape[0]
    layer_out, stack_part, local_grad, back, qkv_grad = pl.pallas_call(
        functools.partial(layer_kernel, scales, bound),
        grid_spec=pltpu.PrefetchScalarGridSpec(
            num_scalar_prefetch=1,
            grid=(tiles // STEP_TILES,),
            in_specs=[
                whole(nodes, width),
                whole(nodes, width),
                whole(devices * bound, width),
                whole(2 * width, width),
                whole(stack, width),
                whole(width, 3 * width),
                pl.BlockSpec((STEP_TILES, RELS, 4, TILE, TILE), lambda i, index: (i, 0, 0, 0, 0)),
            ],
            out_specs=(
                pl.BlockSpec((rows, width), lambda i, index: (i, 0)),
                whole(stack, width),
                whole(nodes, width),
                whole(*packed),
                whole(width, 3 * width),
            ),
            scratch_shapes=[
                pltpu.VMEM((span + 1, TILE, width), BF16),
                pltpu.VMEM((span + 1, width, TILE), F32),
                pltpu.VMEM((rows, stack), BF16),
                pltpu.VMEM((width, width), BF16),
                pltpu.VMEM((width, width), BF16),
            ],
        ),
        out_shape=(
            jax.ShapeDtypeStruct((nodes, width), BF16),
            jax.ShapeDtypeStruct((stack, width), F32),
            jax.ShapeDtypeStruct((nodes, width), F32),
            jax.ShapeDtypeStruct(packed, BF16),
            jax.ShapeDtypeStruct((width, 3 * width), F32),
        ),
        compiler_params=pltpu.CompilerParams(
            dimension_semantics=("arbitrary",), vmem_limit_bytes=VMEM_LIMIT
        ),
        name="layer",
    )(index, features, cotangent, halo, moments, w_stack, w_qkv, tile_values)

    stack_grad, input_grad = pl.pallas_call(
        functools.partial(return_kernel, shape),
        out_shape=(
            jax.ShapeDtypeStruct((stack, width), F32),
            jax.ShapeDtypeStruct((nodes, width), BF16),
        ),
        in_specs=[in_vmem] * 4,
        out_specs=(in_vmem, in_vmem),
        scratch_shapes=[
            pltpu.VMEM(packed, BF16),
            pltpu.SemaphoreType.DMA((devices,)),
            pltpu.SemaphoreType.DMA((devices,)),
            pltpu.VMEM((stack, width), BF16),
            *sum_scratch(stack, width, row_count, col_count),
        ],
        compiler_params=pltpu.CompilerParams(
            collective_id=1, has_side_effects=True, vmem_limit_bytes=VMEM_LIMIT
        ),
        name="giveback",
    )(stack_part, back, local_grad, send_rows.reshape(1, devices * bound))
    return layer_out, input_grad, stack_grad, qkv_grad


def solution(mesh):
    both = ("row", "col")
    placed = (
        P(both, None),
        P(both, None),
        P(both, None, None, None, None),
        P(both, None, None),
        P(both, None),
        P(both, None, None),
        P(),
        P(),
    )
    return jax.shard_map(
        functools.partial(local, mesh.shape["row"], mesh.shape["col"]),
        mesh=mesh,
        in_specs=placed,
        out_specs=(P(both, None), P(both, None), P(), P()),
        check_vma=False,
    )
```

```python
import functools

import jax
import jax.numpy as jnp
from jax import lax
from jax.experimental import pallas as pl
from jax.experimental.pallas import tpu as pltpu
from jax.sharding import PartitionSpec as P

HEADS = 4
RELS = 4
TILE = 128
MESH = pl.DeviceIdType.MESH
BF16 = jnp.bfloat16
F32 = jnp.float32
VMEM_LIMIT = 48 * 1024 * 1024
STEP_TILES = 2


def dot(a, b, dims=((1,), (0,)), precision=None):
    return lax.dot_general(a, b, (dims, ((), ())), preferred_element_type=F32, precision=precision)


def pack_rows(rows, bound):
    count, width = rows.shape
    left = rows[:, : width // 2].reshape(count // bound, bound, width // 2)
    right = rows[:, width // 2 :].reshape(count // bound, bound, width // 2)
    return jnp.concatenate([left, right], axis=1)


def unpack_rows(packed, bound):
    count, _, half = packed.shape
    left = packed[:, :bound].reshape(count * bound, half)
    right = packed[:, bound:].reshape(count * bound, half)
    return jnp.concatenate([left, right], axis=1)


class Place:
    def __init__(self, rows, cols):
        self.rows, self.cols, self.planes = rows, cols, cols // 2
        self.devices = rows * cols
        self.row, self.col = lax.axis_index("row"), lax.axis_index("col")
        self.me = self.row * cols + self.col
        self.core = lax.rem(self.col, 2)
        self.plane = lax.div(self.col, 2)

    def peer(self, offset):
        other = lax.rem(self.me + offset, self.devices)
        return (lax.div(other, self.cols), lax.rem(other, self.cols))

    def greet(self):
        barrier = pltpu.get_barrier_semaphore()

        def signal(offset, carry):
            pl.semaphore_signal(barrier, inc=1, device_id=self.peer(offset), device_id_type=MESH)
            return carry

        lax.fori_loop(1, self.devices, signal, 0)

    def met(self):
        pl.semaphore_wait(pltpu.get_barrier_semaphore(), self.devices - 1)


def exchange_copy(place, offset, out, into, sends, recvs):
    other = lax.rem(place.me + offset, place.devices)
    return pltpu.make_async_remote_copy(
        src_ref=out.at[other],
        dst_ref=into.at[place.me],
        send_sem=sends.at[offset],
        recv_sem=recvs.at[offset],
        device_id=place.peer(offset),
        device_id_type=MESH,
    )


def exchange_start(place, out, into, sends, recvs):
    into[place.me] = out[place.me]

    def start(offset, carry):
        exchange_copy(place, offset, out, into, sends, recvs).start()
        return carry

    lax.fori_loop(1, place.devices, start, 0)


def exchange_wait(place, out, into, sends, recvs):
    def wait(offset, carry):
        exchange_copy(place, offset, out, into, sends, recvs).wait()
        return carry

    lax.fori_loop(1, place.devices, wait, 0)


def row_share(rows, row_count, col_count, kind):
    chunk = rows // col_count
    align = 16 if kind == BF16 else 8
    return chunk // row_count if chunk % (row_count * align) == 0 else 0


def sum_scratch(rows, width, row_count, col_count, kind):
    half, chunk, planes = rows // 2, rows // col_count, col_count // 2
    share = row_share(rows, row_count, col_count, kind)
    count = 1 + 2 * (planes - 1) + 2 * (row_count - 1) + planes
    return [
        pltpu.VMEM((half, width), kind),
        pltpu.VMEM((half, width), kind),
        pltpu.VMEM((half, width), kind),
        pltpu.VMEM((planes, chunk, width), kind),
        pltpu.VMEM((chunk, width), kind),
        pltpu.VMEM((row_count, share or chunk, width), kind),
        pltpu.SemaphoreType.DMA((count,)),
        pltpu.SemaphoreType.DMA((count,)),
    ]


def sum_all(place, part, out, scratch):
    out0, in0, out1, in1, out2, in2, sends, recvs = scratch
    kind = out.dtype
    rows = part.shape[0]
    half, chunk = rows // 2, rows // place.cols
    share = row_share(rows, place.rows, place.cols, kind)
    core, plane, row, planes = place.core, place.plane, place.row, place.planes
    partner = (row, place.col + 1 - 2 * core)
    used = [0]

    def copy(src, dst, device):
        index = used[0]
        used[0] += 1
        moved = pltpu.make_async_remote_copy(
            src_ref=src, dst_ref=dst, send_sem=sends.at[index], recv_sem=recvs.at[index],
            device_id=device, device_id_type=MESH,
        )
        moved.start()
        return moved

    out0[...] = part[pl.ds(pl.multiple_of((1 - core) * half, 16), half), :].astype(kind)
    first = copy(out0, in0, partner)
    yield
    first.wait()
    mine = part[pl.ds(pl.multiple_of(core * half, 16), half), :]
    out1[...] = (mine + in0[...].astype(F32)).astype(kind)

    def piece(index, size=chunk):
        return pl.ds(pl.multiple_of(index * size, 8), size)

    copies = []
    for step in range(1, planes):
        other = lax.rem(plane + step, planes)
        copies.append(copy(out1.at[piece(other), :], in1.at[step], (row, other * 2 + core)))
    yield
    total = out1[piece(plane), :].astype(F32)
    for step in range(1, planes):
        copies[step - 1].wait()
        total = total + in1[step].astype(F32)

    def spot(index):
        return pl.ds(pl.multiple_of(core * half + index * chunk, 8), chunk)

    out2[...] = total.astype(kind)
    others = [lax.rem(row + step, place.rows) for step in range(1, place.rows)]
    if share:
        copies = [
            copy(out2.at[piece(other, share), :], in2.at[step], (other, place.col))
            for step, other in enumerate(others)
        ]
        yield
        total = out2[piece(row, share), :].astype(F32)
        for step, moved in enumerate(copies):
            moved.wait()
            total = total + in2[step].astype(F32)
        part_spot = pl.ds(pl.multiple_of(core * half + plane * chunk + row * share, 8), share)
        out[part_spot, :] = total.astype(kind)
        copies = [copy(out.at[part_spot, :], out.at[part_spot, :], (other, place.col)) for other in others]
        yield
        for moved in copies:
            moved.wait()
    else:
        in2[row] = out2[...]
        copies = [copy(out2, in2.at[row], (other, place.col)) for other in others]
        yield
        for moved in copies:
            moved.wait()
        total = in2[0].astype(F32)
        for step in range(1, place.rows):
            total = total + in2[step].astype(F32)
        out[spot(plane), :] = total.astype(kind)

    mine = out.at[spot(plane), :]
    copies = []
    for step in range(1, planes):
        other = lax.rem(plane + step, planes)
        copies.append(copy(mine, mine, (row, other * 2 + core)))
    passed = [copy(mine, mine, partner)]
    yield
    for step in range(1, planes):
        copies[step - 1].wait()
        source = spot(lax.rem(plane - step + planes, planes))
        passed.append(copy(out.at[source, :], out.at[source, :], partner))
    yield
    for moved in passed:
        moved.wait()


def gather_kernel(shape, f_ref, c_ref, rows_ref, halo_ref, moments_ref, outgoing, incoming, sends, recvs):
    row_count, col_count, bound = shape
    place = Place(row_count, col_count)
    place.greet()
    nodes, width = f_ref.shape
    block = 512
    wanted = rows_ref[...]
    picked = jnp.zeros((wanted.shape[0], width), F32)
    for at in range(0, nodes, block):
        spots = lax.broadcasted_iota(jnp.int32, (wanted.shape[0], block), 1) + at
        picked += dot(jnp.where(spots == wanted, 1.0, 0.0).astype(BF16), f_ref[at : at + block, :])
    outgoing[...] = pack_rows(picked, bound).astype(BF16)
    place.met()
    exchange_start(place, outgoing, incoming, sends, recvs)
    gram = jnp.zeros((width, width), F32)
    cross = jnp.zeros((width, width), F32)
    for at in range(0, nodes, block):
        f = f_ref[at : at + block, :]
        gram += dot(f, f, ((0,), (0,)))
        cross += dot(f, c_ref[at : at + block, :], ((0,), (0,)))
    moments_ref[:width, :] = gram
    moments_ref[width:, :] = cross
    exchange_wait(place, outgoing, incoming, sends, recvs)
    halo_ref[...] = unpack_rows(incoming[...].astype(F32), bound).astype(BF16)


def layer_kernel(
    bound, index_ref, f_ref, c_ref, halo_ref, w_ref, tv_ref,
    act_ref, stack_ref, local_ref, back_ref, ext, ext_grad, joined,
):
    step = pl.program_id(0)
    nodes, width = f_ref.shape
    tiles = nodes // TILE
    span = ext.shape[0] - 1

    @pl.when(step == 0)
    def _():
        for t in range(tiles):
            ext[t] = f_ref[t * TILE : (t + 1) * TILE, :]
        for t in range(tiles, span):
            ext[t] = halo_ref[(t - tiles) * TILE : (t - tiles + 1) * TILE, :]
        ext[span] = jnp.zeros((TILE, width), BF16)
        ext_grad[...] = jnp.zeros_like(ext_grad)
        stack_ref[...] = jnp.zeros_like(stack_ref)

    rows = STEP_TILES * TILE
    here = pl.ds(pl.multiple_of(step * rows, rows), rows)
    feats, cots = f_ref[here, :], c_ref[here, :]
    joined[:, :width] = feats

    def slot(tile, relation, s):
        return index_ref[((step * STEP_TILES + tile) * RELS + relation) * 4 + s]

    def adjacency(tile, relation):
        return jnp.concatenate([tv_ref[tile, relation, s] for s in range(4)], axis=1)

    for tile in range(STEP_TILES):
        for relation in range(RELS):
            source = jnp.concatenate([ext[slot(tile, relation, s)] for s in range(4)], axis=0)
            message = dot(adjacency(tile, relation), source)
            joined[tile * TILE : (tile + 1) * TILE, (relation + 1) * width : (relation + 2) * width] = message.astype(BF16)
    pre = dot(joined[...], w_ref[...])
    root = 0.7978845608028654
    square = pre * pre
    bent = jnp.tanh(root * pre * (1.0 + 0.044715 * square))
    upper = 0.5 * (1.0 + bent)
    slope = upper + 0.5 * pre * (1.0 - bent * bent) * root * (1.0 + 3 * 0.044715 * square)
    grad_pre = (cots.astype(F32) * slope).astype(BF16)
    act_ref[...] = pre * upper
    stack = w_ref.shape[0]
    weight = dot(joined[...], grad_pre, ((0,), (0,)))
    stack_ref[:stack, :] += weight[:, : width // 2]
    stack_ref[stack:, :] += weight[:, width // 2 :]
    own = dot(w_ref[:width, :], grad_pre, ((1,), (1,)))
    for tile in range(STEP_TILES):
        ext_grad[step * STEP_TILES + tile] += own[:, tile * TILE : (tile + 1) * TILE]
    for relation in range(RELS):
        pulled = dot(w_ref[(relation + 1) * width : (relation + 2) * width, :], grad_pre, ((1,), (1,))).astype(BF16)
        for tile in range(STEP_TILES):
            spread = dot(pulled[:, tile * TILE : (tile + 1) * TILE], adjacency(tile, relation))
            for s in range(4):
                ext_grad[slot(tile, relation, s)] += spread[:, s * TILE : (s + 1) * TILE]

    @pl.when(step == pl.num_programs(0) - 1)
    def _():
        for t in range(tiles):
            local_ref[t * TILE : (t + 1) * TILE, :] = ext_grad[t].T
        group = TILE // bound
        for t in range(tiles, span):
            back_ref[(t - tiles) * group : (t - tiles + 1) * group] = pack_rows(ext_grad[t].T, bound).astype(BF16)


def split(value):
    high = value.astype(BF16)
    return high, (value - high.astype(F32)).astype(BF16)


def dot_wide(a, b, dims=((1,), (0,))):
    if a.dtype == BF16:
        b_high, b_low = split(b)
        return dot(a, b_high, dims) + dot(a, b_low, dims)
    if b.dtype == BF16:
        a_high, a_low = split(a)
        return dot(a_high, b, dims) + dot(a_low, b, dims)
    a_high, a_low = split(a)
    b_high, b_low = split(b)
    return dot(a_high, b_high, dims) + (dot(a_high, b_low, dims) + dot(a_low, b_high, dims))


def finish(scales, moments, wqkv, feats, cots, act, held, loads, landed, rows_ref, out_ref, grad_ref, qkv_ref):
    node_scale, head_scale = scales
    nodes, width = feats.shape
    head = width // HEADS
    gram, cross = moments[:width, :], moments[width:, :]
    w_q, w_k, w_v = (wqkv[:, at * width : (at + 1) * width] for at in range(3))
    same = lax.div(lax.broadcasted_iota(jnp.int32, (width, width), 0), head) == lax.div(
        lax.broadcasted_iota(jnp.int32, (width, width), 1), head
    )
    gram_v, gram_k = dot_wide(gram, w_v), dot_wide(gram, w_k)
    state = jnp.where(same, dot_wide(w_k, gram_v, ((0,), (0,))), 0.0) * node_scale
    state_grad = jnp.where(same, dot_wide(w_q, cross, ((0,), (0,))), 0.0) * head_scale
    yield
    mix = (dot_wide(w_q, state) * head_scale).astype(BF16)
    turned = dot_wide(dot_wide(w_k, state_grad), w_v, ((1,), (1,)))
    sym = ((turned + turned.T) * node_scale).astype(BF16)
    yield
    qkv_ref[:, :width] = dot_wide(cross, state, ((1,), (1,))) * head_scale
    qkv_ref[:, width : 2 * width] = dot_wide(gram_v, state_grad, ((1,), (1,))) * node_scale
    qkv_ref[:, 2 * width :] = dot_wide(gram_k, state_grad) * node_scale
    for load in loads:
        load.wait()
    returned = landed()
    yield
    wanted = rows_ref[...]
    block = 512
    for at in range(0, nodes, block):
        here = slice(at, at + block)
        spots = lax.broadcasted_iota(jnp.int32, (block, wanted.shape[1]), 0) + at
        spread = dot(jnp.where(spots == wanted, 1.0, 0.0).astype(BF16), returned)
        out_ref[here, :] = (act[here, :] + dot(feats[here, :], mix)).astype(BF16)
        attention = dot(cots[here, :], mix, ((1,), (1,))) + dot(feats[here, :], sym)
        grad_ref[here, :] = (held[here, :] + spread + attention).astype(BF16)
        yield


def return_kernel(
    shape, scales, streams, moments_in, stack_in, back_in, rows_ref, wqkv, f_in, c_in, act_in, local_in,
    stack_ref, grad_ref, out_ref, qkv_ref,
    incoming, sends, recvs, load_sems, feats, cots, act, held, total, moments, *scratch,
):
    row_count, col_count, bound = shape
    place = Place(row_count, col_count)
    place.greet()
    loads = []
    for at, (src, dst) in enumerate(((f_in, feats), (c_in, cots), (act_in, act), (local_in, held))):
        loads.append(pltpu.make_async_copy(src, dst, load_sems.at[at]))
        loads[-1].start()
    place.met()
    exchange_start(place, back_in, incoming, sends, recvs)

    def landed():
        exchange_wait(place, back_in, incoming, sends, recvs)
        return unpack_rows(incoming[...].astype(F32), bound).astype(BF16)

    early = sum_all(place, moments_in, moments, scratch[:streams])
    late = sum_all(place, stack_in, total, scratch[streams:])
    done = object()
    next(early)
    while next(early, done) is not done:
        next(late, done)
    work = finish(scales, moments, wqkv, feats, cots, act, held, loads, landed, rows_ref, out_ref, grad_ref, qkv_ref)
    active = [work, late]
    while active:
        active = [steps for steps in active if next(steps, done) is not done]
    stack = stack_ref.shape[0]
    stack_ref[...] = jnp.concatenate([total[:stack, :], total[stack:, :]], axis=1)


def local(row_count, col_count, features, cotangent, tile_values, tile_src, tile_count, send_rows, w_stack, w_qkv):
    nodes, width = features.shape
    devices = row_count * col_count
    bound = send_rows.shape[2]
    tiles = nodes // TILE
    span = tiles + devices * bound // TILE
    slots = lax.broadcasted_iota(jnp.int32, tile_src.shape, 2)
    index = jnp.where(slots < tile_count[:, :, None], tile_src, span).reshape(-1)
    shape = (row_count, col_count, bound)
    in_vmem = pl.BlockSpec(memory_space=pltpu.VMEM)
    packed = (devices, 2 * bound, width // 2)

    stack = w_stack.shape[0]
    scales = (float(nodes * devices) ** -0.5, float(width // HEADS) ** -0.5)
    halo, moments = pl.pallas_call(
        functools.partial(gather_kernel, shape),
        out_shape=(
            jax.ShapeDtypeStruct((devices * bound, width), BF16),
            jax.ShapeDtypeStruct((2 * width, width), F32),
        ),
        in_specs=[in_vmem] * 3,
        out_specs=(in_vmem, in_vmem),
        scratch_shapes=[
            pltpu.VMEM(packed, BF16),
            pltpu.VMEM(packed, BF16),
            pltpu.SemaphoreType.DMA((devices,)),
            pltpu.SemaphoreType.DMA((devices,)),
        ],
        compiler_params=pltpu.CompilerParams(
            collective_id=0, has_side_effects=True, vmem_limit_bytes=VMEM_LIMIT
        ),
        name="gather",
    )(features, cotangent, send_rows.reshape(devices * bound, 1))

    rows = STEP_TILES * TILE
    whole = lambda *dims: pl.BlockSpec(dims, lambda i, index: (0,) * len(dims))
    by_rows = pl.BlockSpec((rows, width), lambda i, index: (i, 0))
    act, stack_part, local_grad, back = pl.pallas_call(
        functools.partial(layer_kernel, bound),
        grid_spec=pltpu.PrefetchScalarGridSpec(
            num_scalar_prefetch=1,
            grid=(tiles // STEP_TILES,),
            in_specs=[
                whole(nodes, width),
                whole(nodes, width),
                whole(devices * bound, width),
                whole(stack, width),
                pl.BlockSpec((STEP_TILES, RELS, 4, TILE, TILE), lambda i, index: (i, 0, 0, 0, 0)),
            ],
            out_specs=(
                by_rows,
                whole(2 * stack, width // 2),
                whole(nodes, width),
                whole(*packed),
            ),
            scratch_shapes=[
                pltpu.VMEM((span + 1, TILE, width), BF16),
                pltpu.VMEM((span + 1, width, TILE), F32),
                pltpu.VMEM((rows, stack), BF16),
            ],
        ),
        out_shape=(
            jax.ShapeDtypeStruct((nodes, width), F32),
            jax.ShapeDtypeStruct((2 * stack, width // 2), F32),
            jax.ShapeDtypeStruct((nodes, width), F32),
            jax.ShapeDtypeStruct(packed, BF16),
        ),
        compiler_params=pltpu.CompilerParams(
            dimension_semantics=("arbitrary",), vmem_limit_bytes=VMEM_LIMIT
        ),
        name="layer",
    )(index, features, cotangent, halo, w_stack, tile_values)

    moment_scratch = sum_scratch(2 * width, width, row_count, col_count, F32)
    stack_scratch = sum_scratch(2 * stack, width // 2, row_count, col_count, BF16)
    in_any = pl.BlockSpec(memory_space=pl.ANY)
    stack_grad, input_grad, layer_out, qkv_grad = pl.pallas_call(
        functools.partial(return_kernel, shape, scales, len(moment_scratch)),
        out_shape=(
            jax.ShapeDtypeStruct((stack, width), BF16),
            jax.ShapeDtypeStruct((nodes, width), BF16),
            jax.ShapeDtypeStruct((nodes, width), BF16),
            jax.ShapeDtypeStruct((width, 3 * width), F32),
        ),
        in_specs=[in_vmem] * 5 + [in_any] * 4,
        out_specs=(in_vmem,) * 4,
        scratch_shapes=[
            pltpu.VMEM(packed, BF16),
            pltpu.SemaphoreType.DMA((devices,)),
            pltpu.SemaphoreType.DMA((devices,)),
            pltpu.SemaphoreType.DMA((4,)),
            pltpu.VMEM((nodes, width), BF16),
            pltpu.VMEM((nodes, width), BF16),
            pltpu.VMEM((nodes, width), F32),
            pltpu.VMEM((nodes, width), F32),
            pltpu.VMEM((2 * stack, width // 2), BF16),
            pltpu.VMEM((2 * width, width), F32),
            *moment_scratch,
            *stack_scratch,
        ],
        compiler_params=pltpu.CompilerParams(
            collective_id=1, has_side_effects=True, vmem_limit_bytes=VMEM_LIMIT
        ),
        name="giveback",
    )(moments, stack_part, back, send_rows.reshape(1, devices * bound), w_qkv, features, cotangent, act, local_grad)
    return layer_out, input_grad, stack_grad.astype(F32), qkv_grad


def solution(mesh):
    both = ("row", "col")
    placed = (
        P(both, None),
        P(both, None),
        P(both, None, None, None, None),
        P(both, None, None),
        P(both, None),
        P(both, None, None),
        P(),
        P(),
    )
    return jax.shard_map(
        functools.partial(local, mesh.shape["row"], mesh.shape["col"]),
        mesh=mesh,
        in_specs=placed,
        out_specs=(P(both, None), P(both, None), P(), P()),
        check_vma=False,
    )
```

```python
import functools

import jax
import jax.numpy as jnp
from jax import lax
from jax.experimental import pallas as pl
from jax.experimental.pallas import tpu as pltpu
from jax.sharding import PartitionSpec as P

HEADS = 4
RELS = 4
TILE = 128
MESH = pl.DeviceIdType.MESH
BF16 = jnp.bfloat16
F32 = jnp.float32
VMEM_LIMIT = 48 * 1024 * 1024
STEP_TILES = 4


def dot(a, b, dims=((1,), (0,)), precision=None):
    return lax.dot_general(a, b, (dims, ((), ())), preferred_element_type=F32, precision=precision)


def pack_rows(rows, bound):
    count, width = rows.shape
    left = rows[:, : width // 2].reshape(count // bound, bound, width // 2)
    right = rows[:, width // 2 :].reshape(count // bound, bound, width // 2)
    return jnp.concatenate([left, right], axis=1)


def unpack_rows(packed, bound):
    count, _, half = packed.shape
    left = packed[:, :bound].reshape(count * bound, half)
    right = packed[:, bound:].reshape(count * bound, half)
    return jnp.concatenate([left, right], axis=1)


class Place:
    def __init__(self, rows, cols):
        self.rows, self.cols, self.planes = rows, cols, cols // 2
        self.devices = rows * cols
        self.row, self.col = lax.axis_index("row"), lax.axis_index("col")
        self.me = self.row * cols + self.col
        self.core = lax.rem(self.col, 2)
        self.plane = lax.div(self.col, 2)

    def peer(self, offset):
        other = lax.rem(self.me + offset, self.devices)
        return (lax.div(other, self.cols), lax.rem(other, self.cols))

    def greet(self):
        barrier = pltpu.get_barrier_semaphore()

        def signal(offset, carry):
            pl.semaphore_signal(barrier, inc=1, device_id=self.peer(offset), device_id_type=MESH)
            return carry

        lax.fori_loop(1, self.devices, signal, 0)

    def met(self):
        pl.semaphore_wait(pltpu.get_barrier_semaphore(), self.devices - 1)


def exchange_copy(place, offset, out, into, sends, recvs):
    other = lax.rem(place.me + offset, place.devices)
    return pltpu.make_async_remote_copy(
        src_ref=out.at[other],
        dst_ref=into.at[place.me],
        send_sem=sends.at[offset],
        recv_sem=recvs.at[offset],
        device_id=place.peer(offset),
        device_id_type=MESH,
    )


def exchange_start(place, out, into, sends, recvs):
    into[place.me] = out[place.me]

    def start(offset, carry):
        exchange_copy(place, offset, out, into, sends, recvs).start()
        return carry

    lax.fori_loop(1, place.devices, start, 0)


def exchange_wait(place, out, into, sends, recvs):
    def wait(offset, carry):
        exchange_copy(place, offset, out, into, sends, recvs).wait()
        return carry

    lax.fori_loop(1, place.devices, wait, 0)


def row_share(rows, row_count, col_count, kind):
    chunk = rows // col_count
    align = 16 if kind == BF16 else 8
    return chunk // row_count if chunk % (row_count * align) == 0 else 0


def sum_scratch(rows, width, row_count, col_count, kind):
    half, chunk, planes = rows // 2, rows // col_count, col_count // 2
    share = row_share(rows, row_count, col_count, kind)
    count = 1 + 2 * (planes - 1) + 2 * (row_count - 1) + planes
    return [
        pltpu.VMEM((half, width), kind),
        pltpu.VMEM((half, width), kind),
        pltpu.VMEM((half, width), kind),
        pltpu.VMEM((planes, chunk, width), kind),
        pltpu.VMEM((chunk, width), kind),
        pltpu.VMEM((row_count, share or chunk, width), kind),
        pltpu.SemaphoreType.DMA((count,)),
        pltpu.SemaphoreType.DMA((count,)),
    ]


def sum_all(place, part, out, scratch):
    out0, in0, out1, in1, out2, in2, sends, recvs = scratch
    kind = out.dtype
    rows = part.shape[0]
    half, chunk = rows // 2, rows // place.cols
    share = row_share(rows, place.rows, place.cols, kind)
    core, plane, row, planes = place.core, place.plane, place.row, place.planes
    partner = (row, place.col + 1 - 2 * core)
    used = [0]

    def copy(src, dst, device):
        index = used[0]
        used[0] += 1
        moved = pltpu.make_async_remote_copy(
            src_ref=src, dst_ref=dst, send_sem=sends.at[index], recv_sem=recvs.at[index],
            device_id=device, device_id_type=MESH,
        )
        moved.start()
        return moved

    out0[...] = part[pl.ds(pl.multiple_of((1 - core) * half, 16), half), :].astype(kind)
    first = copy(out0, in0, partner)
    yield
    first.wait()
    mine = part[pl.ds(pl.multiple_of(core * half, 16), half), :]
    out1[...] = (mine + in0[...].astype(F32)).astype(kind)

    def piece(index, size=chunk):
        return pl.ds(pl.multiple_of(index * size, 8), size)

    copies = []
    for step in range(1, planes):
        other = lax.rem(plane + step, planes)
        copies.append(copy(out1.at[piece(other), :], in1.at[step], (row, other * 2 + core)))
    yield
    total = out1[piece(plane), :].astype(F32)
    for step in range(1, planes):
        copies[step - 1].wait()
        total = total + in1[step].astype(F32)

    def spot(index):
        return pl.ds(pl.multiple_of(core * half + index * chunk, 8), chunk)

    out2[...] = total.astype(kind)
    others = [lax.rem(row + step, place.rows) for step in range(1, place.rows)]
    if share:
        copies = [
            copy(out2.at[piece(other, share), :], in2.at[step], (other, place.col))
            for step, other in enumerate(others)
        ]
        yield
        total = out2[piece(row, share), :].astype(F32)
        for step, moved in enumerate(copies):
            moved.wait()
            total = total + in2[step].astype(F32)
        part_spot = pl.ds(pl.multiple_of(core * half + plane * chunk + row * share, 8), share)
        out[part_spot, :] = total.astype(kind)
        copies = [copy(out.at[part_spot, :], out.at[part_spot, :], (other, place.col)) for other in others]
        yield
        for moved in copies:
            moved.wait()
    else:
        in2[row] = out2[...]
        copies = [copy(out2, in2.at[row], (other, place.col)) for other in others]
        yield
        for moved in copies:
            moved.wait()
        total = in2[0].astype(F32)
        for step in range(1, place.rows):
            total = total + in2[step].astype(F32)
        out[spot(plane), :] = total.astype(kind)

    mine = out.at[spot(plane), :]
    copies = []
    for step in range(1, planes):
        other = lax.rem(plane + step, planes)
        copies.append(copy(mine, mine, (row, other * 2 + core)))
    passed = [copy(mine, mine, partner)]
    yield
    for step in range(1, planes):
        copies[step - 1].wait()
        source = spot(lax.rem(plane - step + planes, planes))
        passed.append(copy(out.at[source, :], out.at[source, :], partner))
    yield
    for moved in passed:
        moved.wait()


def gather_kernel(shape, f_ref, c_ref, rows_ref, halo_ref, moments_ref, outgoing, incoming, sends, recvs, cots, load_sem):
    row_count, col_count, bound = shape
    place = Place(row_count, col_count)
    place.greet()
    load = pltpu.make_async_copy(c_ref, cots, load_sem)
    load.start()
    nodes, width = f_ref.shape
    block = 512
    turned = jnp.broadcast_to(rows_ref[...].astype(F32), (TILE, rows_ref.shape[1])).T.astype(jnp.int32)
    wanted = jnp.concatenate([turned] * (block // TILE), axis=1)
    picked = jnp.zeros((wanted.shape[0], width), F32)
    for at in range(0, nodes, block):
        spots = lax.broadcasted_iota(jnp.int32, (wanted.shape[0], block), 1) + at
        picked += dot(jnp.where(spots == wanted, 1.0, 0.0).astype(BF16), f_ref[at : at + block, :])
    outgoing[...] = pack_rows(picked, bound).astype(BF16)
    place.met()
    exchange_start(place, outgoing, incoming, sends, recvs)
    gram = jnp.zeros((width, width), F32)
    cross = jnp.zeros((width, width), F32)
    load.wait()
    for at in range(0, nodes, block):
        f = f_ref[at : at + block, :]
        gram += dot(f, f, ((0,), (0,)))
        cross += dot(f, cots[at : at + block, :], ((0,), (0,)))
    moments_ref[:width, :] = gram
    moments_ref[width:, :] = cross
    exchange_wait(place, outgoing, incoming, sends, recvs)
    halo_ref[...] = unpack_rows(incoming[...].astype(F32), bound).astype(BF16)


def layer_kernel(
    bound, index_ref, f_ref, c_ref, halo_ref, w_ref, tv_ref,
    act_ref, stack_ref, ext_grad, back_ref, ext, joined,
):
    step = pl.program_id(0)
    nodes, width = f_ref.shape
    tiles = nodes // TILE
    span = ext.shape[0] - 1

    @pl.when(step == 0)
    def _():
        for t in range(tiles):
            ext[t] = f_ref[t * TILE : (t + 1) * TILE, :]
        for t in range(tiles, span):
            ext[t] = halo_ref[(t - tiles) * TILE : (t - tiles + 1) * TILE, :]
        ext[span] = jnp.zeros((TILE, width), BF16)
        ext_grad[...] = jnp.zeros_like(ext_grad)
        stack_ref[...] = jnp.zeros_like(stack_ref)

    rows = STEP_TILES * TILE
    here = pl.ds(pl.multiple_of(step * rows, rows), rows)
    feats, cots = f_ref[here, :], c_ref[here, :]
    joined[:, :width] = feats

    def slot(tile, relation, s):
        return index_ref[((step * STEP_TILES + tile) * RELS + relation) * 4 + s]

    def adjacency(tile, relation):
        return jnp.concatenate([tv_ref[tile, relation, s] for s in range(4)], axis=1)

    for tile in range(STEP_TILES):
        for relation in range(RELS):
            source = jnp.concatenate([ext[slot(tile, relation, s)] for s in range(4)], axis=0)
            message = dot(adjacency(tile, relation), source)
            joined[tile * TILE : (tile + 1) * TILE, (relation + 1) * width : (relation + 2) * width] = message.astype(BF16)
    pre = dot(joined[...], w_ref[...])
    root = 0.7978845608028654
    square = pre * pre
    bent = jnp.tanh(root * pre * (1.0 + 0.044715 * square))
    upper = 0.5 * (1.0 + bent)
    slope = upper + 0.5 * pre * (1.0 - bent * bent) * root * (1.0 + 3 * 0.044715 * square)
    grad_pre = (cots.astype(F32) * slope).astype(BF16)
    act_ref[...] = pre * upper
    stack = w_ref.shape[0]
    weight = dot(joined[...], grad_pre, ((0,), (0,)))
    stack_ref[:stack, :] += weight[:, : width // 2]
    stack_ref[stack:, :] += weight[:, width // 2 :]
    own = dot(w_ref[:width, :], grad_pre, ((1,), (1,)))
    for tile in range(STEP_TILES):
        ext_grad[step * STEP_TILES + tile] += own[:, tile * TILE : (tile + 1) * TILE]
    for relation in range(RELS):
        pulled = dot(w_ref[(relation + 1) * width : (relation + 2) * width, :], grad_pre, ((1,), (1,))).astype(BF16)
        for tile in range(STEP_TILES):
            spread = dot(pulled[:, tile * TILE : (tile + 1) * TILE], adjacency(tile, relation))
            for s in range(4):
                ext_grad[slot(tile, relation, s)] += spread[:, s * TILE : (s + 1) * TILE]

    @pl.when(step == pl.num_programs(0) - 1)
    def _():
        group = TILE // bound
        for t in range(tiles, span):
            back_ref[(t - tiles) * group : (t - tiles + 1) * group] = pack_rows(ext_grad[t].T, bound).astype(BF16)


def split(value):
    high = value.astype(BF16)
    return high, (value - high.astype(F32)).astype(BF16)


def dot_wide(a, b, dims=((1,), (0,))):
    if a.dtype == BF16:
        b_high, b_low = split(b)
        return dot(a, b_high, dims) + dot(a, b_low, dims)
    if b.dtype == BF16:
        a_high, a_low = split(a)
        return dot(a_high, b, dims) + dot(a_low, b, dims)
    a_high, a_low = split(a)
    b_high, b_low = split(b)
    return dot(a_high, b_high, dims) + (dot(a_high, b_low, dims) + dot(a_low, b_high, dims))


def prepare(held, base, loads, landed, rows_ref):
    for load in loads:
        load.wait()
    returned = landed()
    yield
    wanted = rows_ref[...]
    block = 4 * TILE
    for at in range(0, base.shape[0], block):
        spots = lax.broadcasted_iota(jnp.int32, (block, wanted.shape[1]), 0) + at
        spread = dot(jnp.where(spots == wanted, 1.0, 0.0).astype(BF16), returned)
        own = jnp.concatenate([held[t].T for t in range(at // TILE, (at + block) // TILE)], axis=0)
        base[at : at + block, :] = own + spread
        yield


def finish(scales, moments, wqkv, feats, cots, act, base, out_ref, grad_ref, qkv_ref):
    node_scale, head_scale = scales
    nodes, width = feats.shape
    head = width // HEADS
    gram, cross = moments[:width, :], moments[width:, :]
    w_q, w_k, w_v = (wqkv[:, at * width : (at + 1) * width] for at in range(3))
    same = lax.div(lax.broadcasted_iota(jnp.int32, (width, width), 0), head) == lax.div(
        lax.broadcasted_iota(jnp.int32, (width, width), 1), head
    )
    gram_v, gram_k = dot_wide(gram, w_v), dot_wide(gram, w_k)
    state = jnp.where(same, dot_wide(w_k, gram_v, ((0,), (0,))), 0.0) * node_scale
    state_grad = jnp.where(same, dot_wide(w_q, cross, ((0,), (0,))), 0.0) * head_scale
    yield
    mix = (dot_wide(w_q, state) * head_scale).astype(BF16)
    turned = dot_wide(dot_wide(w_k, state_grad), w_v, ((1,), (1,)))
    sym = ((turned + turned.T) * node_scale).astype(BF16)
    yield
    qkv_ref[:, :width] = dot_wide(cross, state, ((1,), (1,))) * head_scale
    qkv_ref[:, width : 2 * width] = dot_wide(gram_v, state_grad, ((1,), (1,))) * node_scale
    qkv_ref[:, 2 * width :] = dot_wide(gram_k, state_grad) * node_scale
    yield
    block = 512
    for at in range(0, nodes, block):
        here = slice(at, at + block)
        out_ref[here, :] = (act[here, :] + dot(feats[here, :], mix)).astype(BF16)
        attention = dot(cots[here, :], mix, ((1,), (1,))) + dot(feats[here, :], sym)
        grad_ref[here, :] = (base[here, :] + attention).astype(BF16)
        yield


def return_kernel(
    shape, scales, streams, moments_in, stack_in, back_in, rows_ref, wqkv, f_in, c_in, act_in, local_in,
    stack_ref, grad_ref, out_ref, qkv_ref,
    incoming, sends, recvs, load_sems, feats, cots, act, held, base, total, moments, *scratch,
):
    row_count, col_count, bound = shape
    place = Place(row_count, col_count)
    place.greet()
    loads = []
    for at, (src, dst) in enumerate(((f_in, feats), (c_in, cots), (act_in, act), (local_in.at[pl.ds(0, held.shape[0])], held))):
        loads.append(pltpu.make_async_copy(src, dst, load_sems.at[at]))
        loads[-1].start()
    place.met()
    exchange_start(place, back_in, incoming, sends, recvs)

    def landed():
        exchange_wait(place, back_in, incoming, sends, recvs)
        return unpack_rows(incoming[...].astype(F32), bound).astype(BF16)

    early = sum_all(place, moments_in, moments, scratch[:streams])
    late = sum_all(place, stack_in, total, scratch[streams:])
    done = object()
    ready = prepare(held, base, loads, landed, rows_ref)
    next(early)
    next(late)
    while next(early, done) is not done:
        next(late, done)
        next(ready, done)
    for _ in ready:
        pass
    work = finish(scales, moments, wqkv, feats, cots, act, base, out_ref, grad_ref, qkv_ref)
    active = [work, late]
    while active:
        active = [steps for steps in active if next(steps, done) is not done]
    stack = stack_ref.shape[0]
    stack_ref[...] = jnp.concatenate([total[:stack, :], total[stack:, :]], axis=1)


def local(row_count, col_count, features, cotangent, tile_values, tile_src, tile_count, send_rows, w_stack, w_qkv):
    nodes, width = features.shape
    devices = row_count * col_count
    bound = send_rows.shape[2]
    tiles = nodes // TILE
    span = tiles + devices * bound // TILE
    slots = lax.broadcasted_iota(jnp.int32, tile_src.shape, 2)
    index = jnp.where(slots < tile_count[:, :, None], tile_src, span).reshape(-1)
    shape = (row_count, col_count, bound)
    in_vmem = pl.BlockSpec(memory_space=pltpu.VMEM)
    in_any = pl.BlockSpec(memory_space=pl.ANY)
    flat_rows = send_rows.reshape(1, devices * bound)
    packed = (devices, 2 * bound, width // 2)

    stack = w_stack.shape[0]
    scales = (float(nodes * devices) ** -0.5, float(width // HEADS) ** -0.5)
    halo, moments = pl.pallas_call(
        functools.partial(gather_kernel, shape),
        out_shape=(
            jax.ShapeDtypeStruct((devices * bound, width), BF16),
            jax.ShapeDtypeStruct((2 * width, width), F32),
        ),
        in_specs=[in_vmem, in_any, in_vmem],
        out_specs=(in_vmem, in_vmem),
        scratch_shapes=[
            pltpu.VMEM(packed, BF16),
            pltpu.VMEM(packed, BF16),
            pltpu.SemaphoreType.DMA((devices,)),
            pltpu.SemaphoreType.DMA((devices,)),
            pltpu.VMEM((nodes, width), BF16),
            pltpu.SemaphoreType.DMA,
        ],
        compiler_params=pltpu.CompilerParams(
            collective_id=0, has_side_effects=True, vmem_limit_bytes=VMEM_LIMIT
        ),
        name="gather",
    )(features, cotangent, flat_rows)

    rows = STEP_TILES * TILE
    whole = lambda *dims: pl.BlockSpec(dims, lambda i, index: (0,) * len(dims))
    by_rows = pl.BlockSpec((rows, width), lambda i, index: (i, 0))
    act, stack_part, local_grad, back = pl.pallas_call(
        functools.partial(layer_kernel, bound),
        grid_spec=pltpu.PrefetchScalarGridSpec(
            num_scalar_prefetch=1,
            grid=(tiles // STEP_TILES,),
            in_specs=[
                whole(nodes, width),
                whole(nodes, width),
                whole(devices * bound, width),
                whole(stack, width),
                pl.BlockSpec((STEP_TILES, RELS, 4, TILE, TILE), lambda i, index: (i, 0, 0, 0, 0)),
            ],
            out_specs=(
                by_rows,
                whole(2 * stack, width // 2),
                whole(span + 1, width, TILE),
                whole(*packed),
            ),
            scratch_shapes=[
                pltpu.VMEM((span + 1, TILE, width), BF16),
                pltpu.VMEM((rows, stack), BF16),
            ],
        ),
        out_shape=(
            jax.ShapeDtypeStruct((nodes, width), F32),
            jax.ShapeDtypeStruct((2 * stack, width // 2), F32),
            jax.ShapeDtypeStruct((span + 1, width, TILE), F32),
            jax.ShapeDtypeStruct(packed, BF16),
        ),
        compiler_params=pltpu.CompilerParams(
            dimension_semantics=("arbitrary",), vmem_limit_bytes=VMEM_LIMIT
        ),
        name="layer",
    )(index, features, cotangent, halo, w_stack, tile_values)

    moment_scratch = sum_scratch(2 * width, width, row_count, col_count, F32)
    stack_scratch = sum_scratch(2 * stack, width // 2, row_count, col_count, BF16)
    stack_grad, input_grad, layer_out, qkv_grad = pl.pallas_call(
        functools.partial(return_kernel, shape, scales, len(moment_scratch)),
        out_shape=(
            jax.ShapeDtypeStruct((stack, width), BF16),
            jax.ShapeDtypeStruct((nodes, width), BF16),
            jax.ShapeDtypeStruct((nodes, width), BF16),
            jax.ShapeDtypeStruct((width, 3 * width), F32),
        ),
        in_specs=[in_vmem] * 5 + [in_any] * 4,
        out_specs=(in_vmem,) * 4,
        scratch_shapes=[
            pltpu.VMEM(packed, BF16),
            pltpu.SemaphoreType.DMA((devices,)),
            pltpu.SemaphoreType.DMA((devices,)),
            pltpu.SemaphoreType.DMA((4,)),
            pltpu.VMEM((nodes, width), BF16),
            pltpu.VMEM((nodes, width), BF16),
            pltpu.VMEM((nodes, width), F32),
            pltpu.VMEM((tiles, width, TILE), F32),
            pltpu.VMEM((nodes, width), F32),
            pltpu.VMEM((2 * stack, width // 2), BF16),
            pltpu.VMEM((2 * width, width), F32),
            *moment_scratch,
            *stack_scratch,
        ],
        compiler_params=pltpu.CompilerParams(
            collective_id=1, has_side_effects=True, vmem_limit_bytes=VMEM_LIMIT
        ),
        name="giveback",
    )(moments, stack_part, back, flat_rows, w_qkv, features, cotangent, act, local_grad)
    return layer_out, input_grad, stack_grad.astype(F32), qkv_grad


def solution(mesh):
    both = ("row", "col")
    placed = (
        P(both, None),
        P(both, None),
        P(both, None, None, None, None),
        P(both, None, None),
        P(both, None),
        P(both, None, None),
        P(),
        P(),
    )
    return jax.shard_map(
        functools.partial(local, mesh.shape["row"], mesh.shape["col"]),
        mesh=mesh,
        in_specs=placed,
        out_specs=(P(both, None), P(both, None), P(), P()),
        check_vma=False,
    )
```
